32 devices in a mesh: section: 8 (over y, x, core), rep: 4 (over z).
Axes of the slice: x: 2, y: 2, z: 4, core: 2. Of those that a mesh axis runs over, the one named last changes fastest.
Arguments:
- features: bfloat16 [8, 128, 2048], P(None, 'rep'), may hold values from -6 to 6
- positions: int32 [8, 128], P(None, 'rep'), may hold values from 0 to 63
- labels: int32 [8, 128], P(None, 'rep'), may hold values 0 or 1
- cross_u: bfloat16 [2, 8, 2048, 256], P(None, 'section'), may hold values from -0.125 to 0.125
- cross_v: bfloat16 [2, 8, 256, 2048], P(None, 'section'), may hold values from -0.1875 to 0.1875
- cross_bias: float32 [2, 8, 2048], P(None, 'section'), may hold values from -2 to 2
- head: float32 [2048], replicated, may hold values from -0.125 to 0.125
- pos_table: float32 [64, 256], replicated, may hold values from -6 to 6
- debias_hidden_weight: float32 [256, 256], replicated, may hold values from -0.375 to 0.375
- debias_tower_bias: float32 [256], replicated, may hold values from -3 to 3
- debias_output_weight: float32 [256], replicated, may hold values from -0.375 to 0.375
Outputs:
- loss: float32 [], replicated
- grad_u: float32 [2, 8, 2048, 256], P(None, 'section')
- grad_v: float32 [2, 8, 256, 2048], P(None, 'section')
- grad_bias: float32 [2, 8, 2048], P(None, 'section')
The draws below stay inside these ranges and needn't reach their ends.
All inputs are finite; a program needn't handle non-finite values. No bound on the sum of `labels` on one device may be relied on, other than what follows from the above.
Results may differ from the reference program's by a relative error of at most 0.04.
Values may be sent and summed in bfloat16 or wider, within the bound.
A program may use at most 128 MiB of HBM per device.

```python
import jax
import jax.numpy as jnp
from jax import lax

D = 2048
R = 256
DT = 256
POSN = 64
N_MB = 8
LOOPS = 2
ROWS = 128
N_SECTION = 8


def with_ends(drawn, key, least, largest):
    longest = drawn.shape.index(max(drawn.shape))
    spots = []
    for shift in (0, 1):
        where = [jax.random.randint(jax.random.fold_in(key, axis), (), 0, length) for axis, length in enumerate(drawn.shape)]
        where[longest] = (where[longest] + shift) % drawn.shape[longest]
        spots.append(tuple(where))
    return drawn.at[spots[0]].set(least).at[spots[1]].set(largest)


def levels(rng, dims, cuts, least, top_value):
    factor_of = 1.0
    for position, parts in cuts:
        heights = jax.random.uniform(jax.random.fold_in(jax.random.fold_in(rng, 6), position), (parts,), jnp.float32, least / len(cuts), top_value / len(cuts))
        factor_of = factor_of * jnp.repeat(jnp.exp(heights), dims[position] // parts).reshape((-1,) + (1,) * (len(dims) - 1 - position))
    return factor_of


def gaussian(own_key, shape, scale, most, pieces=(), kind=jnp.bfloat16):
    array = jax.random.normal(own_key, shape, jnp.float32) * scale
    if len(pieces) > 0:
        array = levels(own_key, shape, pieces, -0.22, 0.18) * array
    return jnp.clip(array, min=-most, max=most).astype(kind)


def setup_inputs(seed: int = 0) -> dict:
    streams_of = jax.random.split(jax.random.key(seed), 12)
    features = gaussian(streams_of[0], (N_MB, ROWS, D), 1.0, 6.0, ((1, 4),))
    positions = with_ends(jax.random.randint(streams_of[1], (N_MB, ROWS), 0, POSN), jax.random.fold_in(streams_of[1], 1), 0, POSN - 1).astype(jnp.int32)
    labels = with_ends((jax.random.randint(streams_of[2], (N_MB, ROWS), 0, 4) < 1).astype(jnp.int32), jax.random.fold_in(streams_of[2], 1), 0, 1)
    cross_u = gaussian(streams_of[3], (LOOPS, N_SECTION, D, R), D ** -0.5, 0.125, ((1, 8),))
    cross_v = gaussian(streams_of[4], (LOOPS, N_SECTION, R, D), (4 * R) ** -0.5, 0.1875, ((1, 8),))
    cross_bias = gaussian(streams_of[5], (LOOPS, N_SECTION, D), 0.3, 2.0, ((1, 8),), jnp.float32)
    head = gaussian(streams_of[6], (D,), D ** -0.5, 0.125, (), jnp.float32)
    pos_table = gaussian(streams_of[7], (POSN, DT), 1.0, 6.0, (), jnp.float32)
    debias_hidden_weight = gaussian(streams_of[8], (DT, DT), DT ** -0.5, 0.375, (), jnp.float32)
    debias_tower_bias = gaussian(streams_of[9], (DT,), 0.5, 3.0, (), jnp.float32)
    debias_output_weight = gaussian(streams_of[10], (DT,), DT ** -0.5, 0.375, (), jnp.float32)
    return dict(features=features, positions=positions, labels=labels, cross_u=cross_u, cross_v=cross_v, cross_bias=cross_bias, head=head, pos_table=pos_table, debias_hidden_weight=debias_hidden_weight, debias_tower_bias=debias_tower_bias, debias_output_weight=debias_output_weight)


EPS = 1e-05

def layer_parts(x, x0, w_up, w_down, shift):
    xf = x.astype(jnp.float32)
    scale = lax.rsqrt(lax.optimization_barrier(jnp.mean(xf * xf, axis=-1, keepdims=True)) + EPS)
    normed = (xf * scale).astype(jnp.bfloat16)
    inner = jnp.dot(normed, w_up, preferred_element_type=jnp.float32).astype(jnp.bfloat16)
    cross = jnp.dot(inner, w_down, preferred_element_type=jnp.float32) + shift
    output = (xf + x0.astype(jnp.float32) * cross).astype(jnp.bfloat16)
    return (xf, scale, normed, inner, output)

def layer_back(grad_out, x0, xf, scale, normed, inner, w_up, w_down):
    gcross = (grad_out.astype(jnp.float32) * x0.astype(jnp.float32)).astype(jnp.bfloat16)
    gshift = lax.optimization_barrier(jnp.sum(gcross.astype(jnp.float32), axis=0))
    gdown = jnp.dot(inner.T, gcross, preferred_element_type=jnp.float32)
    ginner = jnp.dot(gcross, w_down.T, preferred_element_type=jnp.float32).astype(jnp.bfloat16)
    gup = jnp.dot(normed.T, ginner, preferred_element_type=jnp.float32)
    gnormed = jnp.dot(ginner, w_up.T, preferred_element_type=jnp.float32)
    gin = grad_out.astype(jnp.float32) + scale * gnormed - xf * scale ** 3 * lax.optimization_barrier(jnp.mean(gnormed * xf, axis=-1, keepdims=True))
    return (gin.astype(jnp.bfloat16), gup, gdown, gshift)

def reference(features, positions, labels, cross_u, cross_v, cross_bias, head, pos_table, debias_hidden_weight, debias_tower_bias, debias_output_weight):
    depth = LOOPS * N_SECTION
    ups = cross_u.reshape(depth, D, R)
    downs = cross_v.reshape(depth, R, D)
    shifts = cross_bias.reshape(depth, D)
    total = N_MB * features.shape[1]
    hidden_index = lax.Precision.HIGHEST

    def micro_step(carry, inputs):
        loss_sum, gu, gv, gb = carry
        x0, pos, lab = inputs

        def forward(x, weights):
            w_up, w_down, shift = weights
            return (layer_parts(x, x0, w_up, w_down, shift)[4], x)
        xl, stash = lax.scan(forward, x0, (ups, downs, shifts))
        onehot = (pos[:, None] == jnp.arange(POSN, dtype=jnp.int32)[None, :]).astype(jnp.float32)
        embedded_rows = jnp.dot(onehot, pos_table, precision=hidden_index)
        hidden_state = jax.nn.relu(jnp.dot(embedded_rows, debias_hidden_weight, precision=hidden_index) + debias_tower_bias)
        click_logit = jnp.dot(xl.astype(jnp.float32), head, precision=hidden_index) + jnp.dot(hidden_state, debias_output_weight, precision=hidden_index)
        labf = lab.astype(jnp.float32)
        loss_part = jnp.sum(jax.nn.softplus(click_logit) - labf * click_logit)
        dlogit = (jax.nn.sigmoid(click_logit) - labf) / total
        dfinal = (dlogit[:, None] * head[None, :]).astype(jnp.bfloat16)

        def backward(grad, weights):
            w_up, w_down, shift, x = weights
            xf, scale, normed, inner, unused = layer_parts(x, x0, w_up, w_down, shift)
            gin, gup, gdown, gshift = layer_back(grad, x0, xf, scale, normed, inner, w_up, w_down)
            return (gin, (gup, gdown, gshift))
        unused_grad, grads = lax.scan(backward, dfinal, (ups, downs, shifts, stash), reverse=True)
        return ((loss_sum + loss_part, gu + grads[0], gv + grads[1], gb + grads[2]), None)
    init = (jnp.zeros((), jnp.float32), jnp.zeros((depth, D, R), jnp.float32), jnp.zeros((depth, R, D), jnp.float32), jnp.zeros((depth, D), jnp.float32))
    result, unused_out = lax.scan(micro_step, init, (features, positions, labels))
    loss_sum, gu, gv, gb = result
    return (loss_sum / total, gu.reshape(LOOPS, N_SECTION, D, R), gv.reshape(LOOPS, N_SECTION, R, D), gb.reshape(LOOPS, N_SECTION, D))
```

```python
import functools

import jax
import jax.numpy as jnp
from jax import lax
from jax.experimental import pallas as pl
from jax.experimental.pallas import tpu as pltpu
from jax.sharding import PartitionSpec as P

EPS = 1e-05
MESH = pl.DeviceIdType.MESH
NN = (((1,), (0,)), ((), ()))
NT = (((1,), (1,)), ((), ()))
TN = (((0,), (0,)), ((), ()))


def dot(a, b, dims):
    return lax.dot_general(a, b, dims, preferred_element_type=jnp.float32)


def kernel(
    total,
    feat,
    pos,
    lab,
    u,
    v,
    bias,
    head,
    table,
    hidden_w,
    tower_b,
    out_w,
    gu,
    gv,
    gb,
    loss,
    xs,
    outs,
    normed,
    inner,
    scales,
    gs,
    gouts,
    gcross,
    ginner,
    tower,
    labcol,
    loss_rows,
    fsend,
    frecv,
    bsend,
    brecv,
):
    micro, rows, width = feat.shape
    loops = u.shape[0]
    sections = lax.axis_size("section")
    section = lax.axis_index("section")
    after = lax.rem(section + 1, sections)
    before = lax.rem(section + sections - 1, sections)
    is_first = section == 0
    is_last = section == sections - 1
    first = jnp.where(is_first, 1, 0)
    last = jnp.where(is_last, 1, 0)

    barrier = pltpu.get_barrier_semaphore()
    for neighbour in (before, after):
        pl.semaphore_signal(
            barrier, inc=1, device_id={"section": neighbour}, device_id_type=MESH
        )

    @pl.when(is_first)
    def _():
        xs[0] = feat[...]

    @pl.when(is_last)
    def _():
        hidden = jax.nn.relu(
            lax.dot_general(
                table[...],
                hidden_w[...],
                NN,
                precision=lax.Precision.HIGHEST,
                preferred_element_type=jnp.float32,
            )
            + tower_b[...]
        )
        by_pos = jnp.sum(hidden * out_w[...], axis=1, keepdims=True)
        places = by_pos.shape[0]
        square = (rows, rows)
        eye = lax.broadcasted_iota(jnp.int32, square, 0) == lax.broadcasted_iota(
            jnp.int32, square, 1
        )
        ids = lax.broadcasted_iota(jnp.int32, (places, rows), 0)
        for m in range(micro):
            row = jnp.sum(
                jnp.where(ids == pos[m : m + 1, :], by_pos, 0.0), axis=0, keepdims=True
            )
            tower[m] = jnp.sum(jnp.where(eye, row, 0.0), axis=1, keepdims=True)
            labf = lab[m : m + 1, :].astype(jnp.float32)
            labcol[m] = jnp.sum(jnp.where(eye, labf, 0.0), axis=1, keepdims=True)

    loss_rows[...] = jnp.zeros_like(loss_rows)
    pl.semaphore_wait(barrier, 2)

    def forward_copy(slot, m, to_slot):
        return pltpu.make_async_remote_copy(
            src_ref=outs.at[slot, m],
            dst_ref=xs.at[to_slot, m],
            send_sem=fsend.at[slot, m],
            recv_sem=frecv.at[to_slot, m],
            device_id={"section": after},
            device_id_type=MESH,
        )

    def backward_copy(slot, m, to_slot):
        return pltpu.make_async_remote_copy(
            src_ref=gouts.at[slot, m],
            dst_ref=gs.at[to_slot, m],
            send_sem=bsend.at[slot, m],
            recv_sem=brecv.at[to_slot, m],
            device_id={"section": before},
            device_id_type=MESH,
        )

    def rows_of(m):
        return pl.ds(pl.multiple_of(m * rows, rows), rows)

    def backward(slot, m):
        g = gs[slot, m].astype(jnp.float32)
        gc = (g * feat[m].astype(jnp.float32)).astype(jnp.bfloat16)
        gcross[slot, rows_of(m), :] = gc
        gi = dot(gc, v[slot, 0], NT).astype(jnp.bfloat16)
        ginner[slot, rows_of(m), :] = gi

        @pl.when(jnp.logical_not(is_first & (slot == 0)))
        def _():
            gn = dot(gi, u[slot, 0], NT)
            xf = xs[slot, m].astype(jnp.float32)
            scale = scales[slot, m]
            inside = jnp.mean(gn * xf, axis=-1, keepdims=True)
            gin = g + scale * gn - xf * (scale * scale * scale * inside)
            gouts[slot, m] = gin.astype(jnp.bfloat16)
            backward_copy(slot, m, slot - first).start()

    def forward(t, carry):
        slot, m = t // micro, t % micro

        @pl.when(jnp.logical_not(is_first & (slot == 0)))
        def _():
            forward_copy(slot, m, slot).wait_recv()

        xf = xs[slot, m].astype(jnp.float32)
        scale = lax.rsqrt(jnp.mean(xf * xf, axis=-1, keepdims=True) + EPS)
        scales[slot, m] = scale
        nm = (xf * scale).astype(jnp.bfloat16)
        normed[slot, rows_of(m), :] = nm
        mid = dot(nm, u[slot, 0], NN).astype(jnp.bfloat16)
        inner[slot, rows_of(m), :] = mid
        cross = dot(mid, v[slot, 0], NN) + bias[slot]
        out = (xf + feat[m].astype(jnp.float32) * cross).astype(jnp.bfloat16)
        ends = is_last & (slot == loops - 1)

        @pl.when(jnp.logical_not(ends))
        def _():
            outs[slot, m] = out
            forward_copy(slot, m, slot + last).start()

        @pl.when(ends)
        def _():
            logit = (
                jnp.sum(out.astype(jnp.float32) * head[...], axis=-1, keepdims=True)
                + tower[m]
            )
            labf = labcol[m]
            soft = jnp.maximum(logit, 0.0) + jnp.log1p(jnp.exp(-jnp.abs(logit)))
            loss_rows[...] += soft - labf * logit
            dlogit = (1.0 / (1.0 + jnp.exp(-logit)) - labf) / total
            gs[slot, m] = (dlogit * head[...]).astype(jnp.bfloat16)
            backward(slot, m)

        return carry

    lax.fori_loop(0, loops * micro, forward, 0)

    def weight_grads(slot):
        part = 512
        for c in range(width // part):
            cols = slice(c * part, (c + 1) * part)
            gu[slot, 0, cols, :] = dot(normed[slot, :, cols], ginner[slot], TN).astype(gu.dtype)
            gc = gcross[slot, :, cols]
            gv[slot, 0, :, cols] = dot(inner[slot], gc, TN).astype(gv.dtype)
            gb[slot, :, cols] = jnp.sum(gc.astype(jnp.float32), axis=0, keepdims=True)

    for back in range(loops):
        slot = loops - 1 - back

        def step(m, carry, slot=slot):
            ends = is_last & (slot == loops - 1)

            @pl.when(jnp.logical_not(ends))
            def _():
                backward_copy(slot, m, slot).wait_recv()
                backward(slot, m)

            return carry

        lax.fori_loop(0, micro, step, 0)
        weight_grads(slot)

    def drain(t, carry):
        slot, m = t // micro, t % micro

        @pl.when(jnp.logical_not(is_last & (slot == loops - 1)))
        def _():
            forward_copy(slot, m, slot).wait_send()

        @pl.when(jnp.logical_not(is_first & (slot == 0)))
        def _():
            backward_copy(slot, m, slot).wait_send()

        return carry

    lax.fori_loop(0, loops * micro, drain, 0)
    loss[...] = jnp.broadcast_to(jnp.sum(loss_rows[...], keepdims=True), loss.shape)


def local(
    features,
    positions,
    labels,
    cross_u,
    cross_v,
    cross_bias,
    head,
    pos_table,
    debias_hidden_weight,
    debias_tower_bias,
    debias_output_weight,
):
    micro, rows, width = features.shape
    loops, _, _, rank = cross_u.shape
    total = micro * rows * lax.axis_size("rep")
    bf16, f32 = jnp.bfloat16, jnp.float32
    vmem = pl.BlockSpec(memory_space=pltpu.VMEM)
    act = pltpu.VMEM((loops, micro, rows, width), bf16)
    wide = pltpu.VMEM((loops, micro * rows, width), bf16)
    thin = pltpu.VMEM((loops, micro * rows, rank), bf16)
    sems = pltpu.SemaphoreType.DMA((loops, micro))
    gu, gv, gb, loss = pl.pallas_call(
        functools.partial(kernel, float(total)),
        out_shape=(
            jax.ShapeDtypeStruct(cross_u.shape, bf16),
            jax.ShapeDtypeStruct(cross_v.shape, bf16),
            jax.ShapeDtypeStruct(cross_bias.shape, f32),
            jax.ShapeDtypeStruct((8, 128), f32),
        ),
        in_specs=[vmem] * 11,
        out_specs=(vmem,) * 4,
        scratch_shapes=[
            act,
            act,
            wide,
            thin,
            pltpu.VMEM((loops, micro, rows, 1), f32),
            act,
            act,
            wide,
            thin,
            pltpu.VMEM((micro, rows, 1), f32),
            pltpu.VMEM((micro, rows, 1), f32),
            pltpu.VMEM((rows, 1), f32),
            sems,
            sems,
            sems,
            sems,
        ],
        compiler_params=pltpu.CompilerParams(
            collective_id=0, has_side_effects=True, vmem_limit_bytes=56 * 2**20
        ),
    )(
        features,
        positions,
        labels,
        cross_u,
        cross_v,
        cross_bias,
        head[None, :],
        pos_table,
        debias_hidden_weight,
        debias_tower_bias[None, :],
        debias_output_weight[None, :],
    )
    loss = lax.psum(loss[0, 0], ("section", "rep")) / total
    gu, gv, gb = lax.psum((gu, gv, gb), "rep")
    return (loss, gu.astype(f32), gv.astype(f32), gb)


def solution(mesh):
    return jax.shard_map(
        local,
        mesh=mesh,
        in_specs=(
            P(None, "rep", None),
            P(None, "rep"),
            P(None, "rep"),
            P(None, "section", None, None),
            P(None, "section", None, None),
            P(None, "section", None),
            P(),
            P(),
            P(),
            P(),
            P(),
        ),
        out_specs=(
            P(),
            P(None, "section", None, None),
            P(None, "section", None, None),
            P(None, "section", None),
        ),
        check_vma=False,
    )
```

```python
import functools

import jax
import jax.numpy as jnp
from jax import lax
from jax.experimental import pallas as pl
from jax.experimental.pallas import tpu as pltpu
from jax.sharding import PartitionSpec as P

EPS = 1e-05
PARTS = 16
MESH = pl.DeviceIdType.MESH
NN = (((1,), (0,)), ((), ()))
NT = (((1,), (1,)), ((), ()))
TN = (((0,), (0,)), ((), ()))


def dot(a, b, dims):
    return lax.dot_general(a, b, dims, preferred_element_type=jnp.float32)


def kernel(
    total,
    feat,
    pos,
    lab,
    u,
    v,
    bias,
    head,
    table,
    hidden_w,
    tower_b,
    out_w,
    gu,
    gv,
    gb,
    loss,
    xs,
    outs,
    normed,
    inner,
    scales,
    gs,
    gouts,
    gcross,
    ginner,
    tower,
    labcol,
    loss_rows,
    fsend,
    frecv,
    bsend,
    brecv,
    own_u,
    own_v,
    part_u,
    part_v,
    inn_u,
    inn_v,
    asend,
    precv,
    osend,
    irecv,
    loss_in,
    lsend,
    lrecv,
    small,
    ssend,
    srecv,
):
    micro, rows, width = feat.shape
    loops = u.shape[0]
    sections = lax.axis_size("section")
    section = lax.axis_index("section")
    after = lax.rem(section + 1, sections)
    before = lax.rem(section + sections - 1, sections)
    is_first = section == 0
    is_last = section == sections - 1
    first = jnp.where(is_first, 1, 0)
    last = jnp.where(is_last, 1, 0)

    barrier = pltpu.get_barrier_semaphore()
    for neighbour in (before, after):
        pl.semaphore_signal(
            barrier, inc=1, device_id={"section": neighbour}, device_id_type=MESH
        )
    replicas = lax.axis_size("rep")
    replica = lax.axis_index("rep")
    for step in range(1, replicas):
        pl.semaphore_signal(
            barrier,
            inc=1,
            device_id={"rep": lax.rem(replica + step, replicas)},
            device_id_type=MESH,
        )

    @pl.when(is_first)
    def _():
        xs[0] = feat[...]

    @pl.when(is_last)
    def _():
        hidden = jax.nn.relu(
            lax.dot_general(
                table[...],
                hidden_w[...],
                NN,
                precision=lax.Precision.HIGHEST,
                preferred_element_type=jnp.float32,
            )
            + tower_b[...]
        )
        by_pos = jnp.sum(hidden * out_w[...], axis=1, keepdims=True)
        places = by_pos.shape[0]
        square = (rows, rows)
        eye = lax.broadcasted_iota(jnp.int32, square, 0) == lax.broadcasted_iota(
            jnp.int32, square, 1
        )
        ids = lax.broadcasted_iota(jnp.int32, (places, rows), 0)
        for m in range(micro):
            row = jnp.sum(
                jnp.where(ids == pos[m : m + 1, :], by_pos, 0.0), axis=0, keepdims=True
            )
            tower[m] = jnp.sum(jnp.where(eye, row, 0.0), axis=1, keepdims=True)
            labf = lab[m : m + 1, :].astype(jnp.float32)
            labcol[m] = jnp.sum(jnp.where(eye, labf, 0.0), axis=1, keepdims=True)

    loss_rows[...] = jnp.zeros_like(loss_rows)
    pl.semaphore_wait(barrier, 1 + replicas)

    def forward_copy(slot, m, to_slot):
        return pltpu.make_async_remote_copy(
            src_ref=outs.at[slot, m],
            dst_ref=xs.at[to_slot, m],
            send_sem=fsend.at[slot, m],
            recv_sem=frecv.at[to_slot, m],
            device_id={"section": after},
            device_id_type=MESH,
        )

    def backward_copy(slot, m, to_slot):
        return pltpu.make_async_remote_copy(
            src_ref=gouts.at[slot, m],
            dst_ref=gs.at[to_slot, m],
            send_sem=bsend.at[slot, m],
            recv_sem=brecv.at[to_slot, m],
            device_id={"section": before},
            device_id_type=MESH,
        )

    def rows_of(m):
        return pl.ds(pl.multiple_of(m * rows, rows), rows)

    def backward(slot, m):
        g = gs[slot, m].astype(jnp.float32)
        gc = (g * feat[m].astype(jnp.float32)).astype(jnp.bfloat16)
        gcross[slot, rows_of(m), :] = gc
        gi = dot(gc, v[slot, 0], NT).astype(jnp.bfloat16)
        ginner[slot, rows_of(m), :] = gi

        @pl.when(jnp.logical_not(is_first & (slot == 0)))
        def _():
            gn = dot(gi, u[slot, 0], NT)
            xf = xs[slot, m].astype(jnp.float32)
            scale = scales[slot, m]
            inside = jnp.mean(gn * xf, axis=-1, keepdims=True)
            gin = g + scale * gn - xf * (scale * scale * scale * inside)
            gouts[slot, m] = gin.astype(jnp.bfloat16)
            backward_copy(slot, m, slot - first).start()

    def forward(t, carry):
        slot, m = t // micro, t % micro

        @pl.when(jnp.logical_not(is_first & (slot == 0)))
        def _():
            forward_copy(slot, m, slot).wait_recv()

        xf = xs[slot, m].astype(jnp.float32)
        scale = lax.rsqrt(jnp.mean(xf * xf, axis=-1, keepdims=True) + EPS)
        scales[slot, m] = scale
        nm = (xf * scale).astype(jnp.bfloat16)
        normed[slot, rows_of(m), :] = nm
        mid = dot(nm, u[slot, 0], NN).astype(jnp.bfloat16)
        inner[slot, rows_of(m), :] = mid
        cross = dot(mid, v[slot, 0], NN) + bias[slot]
        out = (xf + feat[m].astype(jnp.float32) * cross).astype(jnp.bfloat16)
        ends = is_last & (slot == loops - 1)

        @pl.when(jnp.logical_not(ends))
        def _():
            outs[slot, m] = out
            forward_copy(slot, m, slot + last).start()

        @pl.when(ends)
        def _():
            logit = (
                jnp.sum(out.astype(jnp.float32) * head[...], axis=-1, keepdims=True)
                + tower[m]
            )
            labf = labcol[m]
            soft = jnp.maximum(logit, 0.0) + jnp.log1p(jnp.exp(-jnp.abs(logit)))
            loss_rows[...] += soft - labf * logit
            dlogit = (1.0 / (1.0 + jnp.exp(-logit)) - labf) / total
            gs[slot, m] = (dlogit * head[...]).astype(jnp.bfloat16)
            backward(slot, m)

        return carry

    lax.fori_loop(0, loops * micro, forward, 0)

    middle_left = (replicas - 1) // 2
    middle_right = middle_left + 1
    on_left = replica <= middle_left
    in_middle = (replica == middle_left) | (replica == middle_right)
    inward = jnp.where(on_left, replica + 1, replica - 1)
    has_outward = (replica > 0) & (replica < replicas - 1)
    outward = jnp.where(on_left, replica - 1, replica + 1)
    outward = jnp.clip(outward, 0, replicas - 1)
    pieces = loops * PARTS
    rank = own_v.shape[1]
    tall_u, tall_v = width // PARTS, rank // PARTS
    lag = jnp.where(in_middle, 3, 5)

    def piece(ref, kind, q):
        tall = (tall_u, tall_v)[kind]
        slot, p = loops - 1 - q // PARTS, q % PARTS
        return ref.at[slot, pl.ds(pl.multiple_of(p * tall, tall), tall), :]

    def rep_copy(kind, q, source, target, send, recv, to):
        return pltpu.make_async_remote_copy(
            src_ref=piece(source, kind, q),
            dst_ref=piece(target, kind, q),
            send_sem=send.at[kind, q],
            recv_sem=recv.at[kind, q],
            device_id={"rep": to},
            device_id_type=MESH,
        )

    own, part, inn, done = (own_u, own_v), (part_u, part_v), (inn_u, inn_v), (gu, gv)

    def to_middle(kind, q):
        return rep_copy(kind, q, own[kind], part[kind], asend, precv, inward)

    def across(kind, q):
        return rep_copy(kind, q, own[kind], inn[kind], asend, irecv, inward)

    def to_ends(kind, q):
        return rep_copy(kind, q, done[kind], inn[kind], osend, irecv, outward)

    def add(a, b):
        return (a.astype(jnp.float32) + b.astype(jnp.float32)).astype(jnp.bfloat16)

    def gather_in(q):
        for kind in range(2):

            @pl.when(has_outward)
            def _(kind=kind):
                to_middle(kind, q).wait_recv()
                mine = piece(own[kind], kind, q)
                mine[...] = add(mine[...], piece(part[kind], kind, q)[...])

            @pl.when(in_middle)
            def _(kind=kind):
                across(kind, q).start()

            @pl.when(jnp.logical_not(in_middle))
            def _(kind=kind):
                to_middle(kind, q).start()

    def give_out(q):
        for kind in range(2):
            across(kind, q).wait_recv()
            arrived = piece(inn[kind], kind, q)[...]
            result = piece(done[kind], kind, q)

            @pl.when(in_middle)
            def _(kind=kind, arrived=arrived, result=result):
                result[...] = add(piece(own[kind], kind, q)[...], arrived)

            @pl.when(jnp.logical_not(in_middle))
            def _(arrived=arrived, result=result):
                result[...] = arrived

            @pl.when(has_outward)
            def _(kind=kind):
                to_ends(kind, q).start()

    def reduce_step(t):
        @pl.when((t >= 1) & (t - 1 < pieces))
        def _():
            gather_in(t - 1)

        @pl.when((t >= lag) & (t - lag < pieces))
        def _():
            give_out(t - lag)

    def weight_grads(slot):
        part = 512
        for c in range(width // part):
            cols = slice(c * part, (c + 1) * part)
            own_u[slot, cols, :] = dot(normed[slot, :, cols], ginner[slot], TN).astype(
                jnp.bfloat16
            )
            gc = gcross[slot, :, cols]
            own_v[slot, :, cols] = dot(inner[slot], gc, TN).astype(jnp.bfloat16)
            small[replica, slot : slot + 1, cols] = jnp.sum(
                gc.astype(jnp.float32), axis=0, keepdims=True
            )

    def loss_copy():
        return pltpu.make_async_remote_copy(
            src_ref=loss_in,
            dst_ref=loss_in,
            send_sem=lsend,
            recv_sem=lrecv,
            device_id={"section": before},
            device_id_type=MESH,
        )

    def small_copy(source, to):
        return pltpu.make_async_remote_copy(
            src_ref=small.at[source],
            dst_ref=small.at[source],
            send_sem=ssend.at[to],
            recv_sem=srecv.at[source],
            device_id={"rep": to},
            device_id_type=MESH,
        )

    beside = micro <= PARTS
    for back in range(loops):
        slot = loops - 1 - back

        def step(m, carry, slot=slot, back=back):
            ends = is_last & (slot == loops - 1)

            @pl.when(jnp.logical_not(ends))
            def _():
                backward_copy(slot, m, slot).wait_recv()
                backward(slot, m)

            if back > 0 and beside:
                reduce_step((back - 1) * micro + m)
            return carry

        lax.fori_loop(0, micro, step, 0)
        if back == 0:

            @pl.when(is_last)
            def _():
                loss_in[...] = jnp.broadcast_to(
                    jnp.sum(loss_rows[...], keepdims=True), loss_in.shape
                )

            @pl.when(jnp.logical_not(is_last))
            def _():
                loss_copy().wait_recv()

            @pl.when(jnp.logical_not(is_first))
            def _():
                loss_copy().start()

        weight_grads(slot)

    small[replica, loops : loops + 1, :] = jnp.broadcast_to(loss_in[:1, :1], (1, width))
    for step in range(1, replicas):
        small_copy(replica, lax.rem(replica + step, replicas)).start()

    def tail(t, carry):
        reduce_step(t)
        return carry

    lax.fori_loop((loops - 1) * micro if beside else 0, pieces + 5, tail, 0)

    def drain(t, carry):
        slot, m = t // micro, t % micro

        @pl.when(jnp.logical_not(is_last & (slot == loops - 1)))
        def _():
            forward_copy(slot, m, slot).wait_send()

        @pl.when(jnp.logical_not(is_first & (slot == 0)))
        def _():
            backward_copy(slot, m, slot).wait_send()

        return carry

    lax.fori_loop(0, loops * micro, drain, 0)

    def drain_rep(q, carry):
        for kind in range(2):
            across(kind, q).wait_send()

            @pl.when(has_outward)
            def _(kind=kind):
                to_ends(kind, q).wait_send()

        return carry

    lax.fori_loop(0, pieces, drain_rep, 0)

    @pl.when(jnp.logical_not(is_first))
    def _():
        loss_copy().wait_send()

    for step in range(1, replicas):
        other = lax.rem(replica + step, replicas)
        small_copy(replica, other).wait_send()
        small_copy(other, replica).wait_recv()
    summed = small[0]
    for r in range(1, replicas):
        summed = summed + small[r]
    for slot in range(loops):
        gb[slot] = summed[slot : slot + 1, :]
    loss[...] = summed[loops : loops + 1, :128] / total


def local(
    features,
    positions,
    labels,
    cross_u,
    cross_v,
    cross_bias,
    head,
    pos_table,
    debias_hidden_weight,
    debias_tower_bias,
    debias_output_weight,
):
    micro, rows, width = features.shape
    loops, _, _, rank = cross_u.shape
    total = micro * rows * lax.axis_size("rep")
    bf16, f32 = jnp.bfloat16, jnp.float32
    vmem = pl.BlockSpec(memory_space=pltpu.VMEM)
    act = pltpu.VMEM((loops, micro, rows, width), bf16)
    wide = pltpu.VMEM((loops, micro * rows, width), bf16)
    thin = pltpu.VMEM((loops, micro * rows, rank), bf16)
    grad_u = pltpu.VMEM((loops, width, rank), bf16)
    grad_v = pltpu.VMEM((loops, rank, width), bf16)
    rep_sems = pltpu.SemaphoreType.DMA((2, loops * PARTS))
    replicas = lax.axis_size("rep")
    sems = pltpu.SemaphoreType.DMA((loops, micro))
    gu, gv, gb, loss = pl.pallas_call(
        functools.partial(kernel, float(total)),
        out_shape=(
            jax.ShapeDtypeStruct((loops, width, rank), bf16),
            jax.ShapeDtypeStruct((loops, rank, width), bf16),
            jax.ShapeDtypeStruct(cross_bias.shape, f32),
            jax.ShapeDtypeStruct((1, 128), f32),
        ),
        in_specs=[vmem] * 11,
        out_specs=(vmem,) * 4,
        scratch_shapes=[
            act,
            act,
            wide,
            thin,
            pltpu.VMEM((loops, micro, rows, 1), f32),
            act,
            act,
            wide,
            thin,
            pltpu.VMEM((micro, rows, 1), f32),
            pltpu.VMEM((micro, rows, 1), f32),
            pltpu.VMEM((rows, 1), f32),
            sems,
            sems,
            sems,
            sems,
            grad_u,
            grad_v,
            grad_u,
            grad_v,
            grad_u,
            grad_v,
            rep_sems,
            rep_sems,
            rep_sems,
            rep_sems,
            pltpu.VMEM((8, 128), f32),
            pltpu.SemaphoreType.DMA,
            pltpu.SemaphoreType.DMA,
            pltpu.VMEM((replicas, loops + 1, width), f32),
            pltpu.SemaphoreType.DMA((replicas,)),
            pltpu.SemaphoreType.DMA((replicas,)),
        ],
        compiler_params=pltpu.CompilerParams(
            collective_id=0, has_side_effects=True, vmem_limit_bytes=56 * 2**20
        ),
    )(
        features,
        positions,
        labels,
        cross_u,
        cross_v,
        cross_bias,
        head[None, :],
        pos_table,
        debias_hidden_weight,
        debias_tower_bias[None, :],
        debias_output_weight[None, :],
    )
    return (loss[0, 0], gu.astype(f32)[:, None], gv.astype(f32)[:, None], gb)


def solution(mesh):
    return jax.shard_map(
        local,
        mesh=mesh,
        in_specs=(
            P(None, "rep", None),
            P(None, "rep"),
            P(None, "rep"),
            P(None, "section", None, None),
            P(None, "section", None, None),
            P(None, "section", None),
            P(),
            P(),
            P(),
            P(),
            P(),
        ),
        out_specs=(
            P(),
            P(None, "section", None, None),
            P(None, "section", None, None),
            P(None, "section", None),
        ),
        check_vma=False,
    )
```

```python
import functools

import jax
import jax.numpy as jnp
from jax import lax
from jax.experimental import pallas as pl
from jax.experimental.pallas import tpu as pltpu
from jax.sharding import PartitionSpec as P

EPS = 1e-05
PARTS = 16
MESH = pl.DeviceIdType.MESH
NN = (((1,), (0,)), ((), ()))
NT = (((1,), (1,)), ((), ()))
TN = (((0,), (0,)), ((), ()))


def dot(a, b, dims):
    return lax.dot_general(a, b, dims, preferred_element_type=jnp.float32)


def kernel(
    total,
    feat,
    pos,
    lab,
    u,
    v,
    bias,
    head,
    table,
    hidden_w,
    tower_b,
    out_w,
    gu,
    gv,
    gb,
    loss,
    xs,
    outs,
    normed,
    inner,
    scales,
    gs,
    gouts,
    gcross,
    ginner,
    tower,
    labcol,
    loss_rows,
    fsend,
    frecv,
    bsend,
    brecv,
    own_u,
    own_v,
    part_u,
    part_v,
    inn_u,
    inn_v,
    asend,
    precv,
    osend,
    irecv,
    loss_in,
    lsend,
    lrecv,
    small,
    ssend,
    srecv,
):
    micro, rows, width = feat.shape
    loops = u.shape[0]
    sections = lax.axis_size("section")
    section = lax.axis_index("section")
    after = lax.rem(section + 1, sections)
    before = lax.rem(section + sections - 1, sections)
    is_first = section == 0
    is_last = section == sections - 1
    first = jnp.where(is_first, 1, 0)
    last = jnp.where(is_last, 1, 0)

    barrier = pltpu.get_barrier_semaphore()
    for neighbour in (before, after):
        pl.semaphore_signal(
            barrier, inc=1, device_id={"section": neighbour}, device_id_type=MESH
        )
    replicas = lax.axis_size("rep")
    replica = lax.axis_index("rep")
    for step in range(1, replicas):
        pl.semaphore_signal(
            barrier,
            inc=1,
            device_id={"rep": lax.rem(replica + step, replicas)},
            device_id_type=MESH,
        )

    @pl.when(is_first)
    def _():
        xs[0] = feat[...]

    @pl.when(is_last)
    def _():
        hidden = jax.nn.relu(
            lax.dot_general(
                table[...],
                hidden_w[...],
                NN,
                precision=lax.Precision.HIGHEST,
                preferred_element_type=jnp.float32,
            )
            + tower_b[...]
        )
        by_pos = jnp.sum(hidden * out_w[...], axis=1, keepdims=True)
        places = by_pos.shape[0]
        square = (rows, rows)
        eye = lax.broadcasted_iota(jnp.int32, square, 0) == lax.broadcasted_iota(
            jnp.int32, square, 1
        )
        ids = lax.broadcasted_iota(jnp.int32, (places, rows), 0)
        for m in range(micro):
            row = jnp.sum(
                jnp.where(ids == pos[m : m + 1, :], by_pos, 0.0), axis=0, keepdims=True
            )
            tower[m] = jnp.sum(jnp.where(eye, row, 0.0), axis=1, keepdims=True)
            labf = lab[m : m + 1, :].astype(jnp.float32)
            labcol[m] = jnp.sum(jnp.where(eye, labf, 0.0), axis=1, keepdims=True)

    loss_rows[...] = jnp.zeros_like(loss_rows)
    pl.semaphore_wait(barrier, 1 + replicas)

    def forward_copy(slot, m, to_slot):
        return pltpu.make_async_remote_copy(
            src_ref=outs.at[slot, m],
            dst_ref=xs.at[to_slot, m],
            send_sem=fsend.at[slot, m],
            recv_sem=frecv.at[to_slot, m],
            device_id={"section": after},
            device_id_type=MESH,
        )

    def backward_copy(slot, m, to_slot):
        return pltpu.make_async_remote_copy(
            src_ref=gouts.at[slot, m],
            dst_ref=gs.at[to_slot, m],
            send_sem=bsend.at[slot, m],
            recv_sem=brecv.at[to_slot, m],
            device_id={"section": before},
            device_id_type=MESH,
        )

    def rows_of(m):
        return pl.ds(pl.multiple_of(m * rows, rows), rows)

    def backward(slot, m):
        g = gs[slot, m].astype(jnp.float32)
        gc = (g * feat[m].astype(jnp.float32)).astype(jnp.bfloat16)
        gcross[slot, rows_of(m), :] = gc
        gi = dot(gc, v[slot, 0], NT).astype(jnp.bfloat16)
        ginner[slot, rows_of(m), :] = gi

        @pl.when(jnp.logical_not(is_first & (slot == 0)))
        def _():
            gn = dot(gi, u[slot, 0], NT)
            xf = xs[slot, m].astype(jnp.float32)
            scale = scales[slot, m]
            inside = jnp.mean(gn * xf, axis=-1, keepdims=True)
            gin = g + scale * gn - xf * (scale * scale * scale * inside)
            gouts[slot, m] = gin.astype(jnp.bfloat16)
            backward_copy(slot, m, slot - first).start()

    def forward(t, carry):
        slot, m = t // micro, t % micro

        @pl.when(jnp.logical_not(is_first & (slot == 0)))
        def _():
            forward_copy(slot, m, slot).wait_recv()

        xf = xs[slot, m].astype(jnp.float32)
        scale = lax.rsqrt(jnp.mean(xf * xf, axis=-1, keepdims=True) + EPS)
        scales[slot, m] = scale
        nm = (xf * scale).astype(jnp.bfloat16)
        normed[slot, rows_of(m), :] = nm
        mid = dot(nm, u[slot, 0], NN).astype(jnp.bfloat16)
        inner[slot, rows_of(m), :] = mid
        cross = dot(mid, v[slot, 0], NN) + bias[slot]
        out = (xf + feat[m].astype(jnp.float32) * cross).astype(jnp.bfloat16)
        ends = is_last & (slot == loops - 1)

        @pl.when(jnp.logical_not(ends))
        def _():
            outs[slot, m] = out
            forward_copy(slot, m, slot + last).start()

        @pl.when(ends)
        def _():
            logit = (
                jnp.sum(out.astype(jnp.float32) * head[...], axis=-1, keepdims=True)
                + tower[m]
            )
            labf = labcol[m]
            soft = jnp.maximum(logit, 0.0) + jnp.log1p(jnp.exp(-jnp.abs(logit)))
            loss_rows[...] += soft - labf * logit
            dlogit = (1.0 / (1.0 + jnp.exp(-logit)) - labf) / total
            gs[slot, m] = (dlogit * head[...]).astype(jnp.bfloat16)
            backward(slot, m)

        return carry

    lax.fori_loop(0, loops * micro, forward, 0)

    middle_left = (replicas - 1) // 2
    middle_right = middle_left + 1
    on_left = replica <= middle_left
    in_middle = (replica == middle_left) | (replica == middle_right)
    inward = jnp.where(on_left, replica + 1, replica - 1)
    has_outward = (replica > 0) & (replica < replicas - 1)
    outward = jnp.where(on_left, replica - 1, replica + 1)
    outward = jnp.clip(outward, 0, replicas - 1)
    pieces = loops * PARTS
    rank = own_v.shape[1]
    tall_u, tall_v = width // PARTS, rank // PARTS
    lag = jnp.where(in_middle, 3, 5)

    def piece(ref, kind, q):
        tall = (tall_u, tall_v)[kind]
        slot, p = loops - 1 - q // PARTS, q % PARTS
        return ref.at[slot, pl.ds(pl.multiple_of(p * tall, tall), tall), :]

    def rep_copy(kind, q, source, target, send, recv, to):
        return pltpu.make_async_remote_copy(
            src_ref=piece(source, kind, q),
            dst_ref=piece(target, kind, q),
            send_sem=send.at[kind, q],
            recv_sem=recv.at[kind, q],
            device_id={"rep": to},
            device_id_type=MESH,
        )

    own, part, inn, done = (own_u, own_v), (part_u, part_v), (inn_u, inn_v), (gu, gv)

    def to_middle(kind, q):
        return rep_copy(kind, q, own[kind], part[kind], asend, precv, inward)

    def across(kind, q):
        return rep_copy(kind, q, own[kind], inn[kind], asend, irecv, inward)

    def to_ends(kind, q):
        return rep_copy(kind, q, done[kind], inn[kind], osend, irecv, outward)

    def add(a, b):
        return (a.astype(jnp.float32) + b.astype(jnp.float32)).astype(jnp.bfloat16)

    def gather_in(q):
        for kind in range(2):

            @pl.when(has_outward)
            def _(kind=kind):
                to_middle(kind, q).wait_recv()
                mine = piece(own[kind], kind, q)
                mine[...] = add(mine[...], piece(part[kind], kind, q)[...])

            @pl.when(in_middle)
            def _(kind=kind):
                across(kind, q).start()

            @pl.when(jnp.logical_not(in_middle))
            def _(kind=kind):
                to_middle(kind, q).start()

    def give_out(q):
        for kind in range(2):
            across(kind, q).wait_recv()
            arrived = piece(inn[kind], kind, q)[...]
            result = piece(done[kind], kind, q)

            @pl.when(in_middle)
            def _(kind=kind, arrived=arrived, result=result):
                result[...] = add(piece(own[kind], kind, q)[...], arrived)

            @pl.when(jnp.logical_not(in_middle))
            def _(arrived=arrived, result=result):
                result[...] = arrived

            @pl.when(has_outward)
            def _(kind=kind):
                to_ends(kind, q).start()

    at_end = jnp.logical_not(has_outward | in_middle)

    def reduce_step(t, ahead=False):
        gathers = (t >= 1) & (t - 1 < pieces)

        @pl.when(gathers & jnp.logical_not(at_end) if ahead else gathers)
        def _():
            gather_in(t - 1)

        @pl.when((t >= lag) & (t - lag < pieces))
        def _():
            give_out(t - lag)

    def send_ahead(start, stop):
        @pl.when(at_end)
        def _():
            def one(q, carry):
                for kind in range(2):
                    to_middle(kind, q).start()
                return carry

            lax.fori_loop(start, stop, one, 0)

    chunks = 4
    chunk = width // chunks

    def weight_grads(slot, then=None):
        def some(c, carry):
            cols = pl.ds(pl.multiple_of(c * chunk, chunk), chunk)
            own_u[slot, cols, :] = dot(normed[slot, :, cols], ginner[slot], TN).astype(
                jnp.bfloat16
            )
            gc = gcross[slot, :, cols]
            own_v[slot, :, cols] = dot(inner[slot], gc, TN).astype(jnp.bfloat16)
            small[replica, slot : slot + 1, cols] = jnp.sum(
                gc.astype(jnp.float32), axis=0, keepdims=True
            )
            if then is not None:
                then(c)
            return carry

        lax.fori_loop(0, chunks, some, 0)

    def loss_copy():
        return pltpu.make_async_remote_copy(
            src_ref=loss_in,
            dst_ref=loss_in,
            send_sem=lsend,
            recv_sem=lrecv,
            device_id={"section": before},
            device_id_type=MESH,
        )

    def small_copy(source, to):
        return pltpu.make_async_remote_copy(
            src_ref=small.at[source],
            dst_ref=small.at[source],
            send_sem=ssend.at[to],
            recv_sem=srecv.at[source],
            device_id={"rep": to},
            device_id_type=MESH,
        )

    beside = loops > 1 and micro + chunks <= PARTS
    for back in range(loops):
        slot = loops - 1 - back

        def step(m, carry, slot=slot, back=back):
            ends = is_last & (slot == loops - 1)

            @pl.when(jnp.logical_not(ends))
            def _():
                backward_copy(slot, m, slot).wait_recv()
                backward(slot, m)

            if back > 0 and beside:
                reduce_step((back - 1) * micro + m)
            return carry

        lax.fori_loop(0, micro, step, 0)
        if back == 0:

            @pl.when(is_last)
            def _():
                loss_in[...] = jnp.broadcast_to(
                    jnp.sum(loss_rows[...], keepdims=True), loss_in.shape
                )

            @pl.when(jnp.logical_not(is_last))
            def _():
                loss_copy().wait_recv()

            @pl.when(jnp.logical_not(is_first))
            def _():
                loss_copy().start()

        if slot > 0:
            weight_grads(slot)

    now = (loops - 1) * micro if beside else 0
    begin = max(now - 1, 0)
    split = pieces - PARTS
    send_ahead(begin, split)
    if loops > 1:
        weight_grads(0, lambda c: reduce_step(now + c, ahead=True))
        now = now + chunks
    else:
        weight_grads(0)
    send_ahead(split, pieces)
    small[replica, loops : loops + 1, :] = jnp.broadcast_to(loss_in[:1, :1], (1, width))
    for step in range(1, replicas):
        small_copy(replica, lax.rem(replica + step, replicas)).start()

    def tail(t, carry):
        reduce_step(t, ahead=True)
        return carry

    lax.fori_loop(now, pieces + 5, tail, 0)

    def drain(t, carry):
        slot, m = t // micro, t % micro

        @pl.when(jnp.logical_not(is_last & (slot == loops - 1)))
        def _():
            forward_copy(slot, m, slot).wait_send()

        @pl.when(jnp.logical_not(is_first & (slot == 0)))
        def _():
            backward_copy(slot, m, slot).wait_send()

        return carry

    lax.fori_loop(0, loops * micro, drain, 0)

    def drain_rep(q, carry):
        for kind in range(2):
            across(kind, q).wait_send()

            @pl.when(has_outward)
            def _(kind=kind):
                to_ends(kind, q).wait_send()

        return carry

    lax.fori_loop(0, pieces, drain_rep, 0)

    @pl.when(jnp.logical_not(is_first))
    def _():
        loss_copy().wait_send()

    for step in range(1, replicas):
        other = lax.rem(replica + step, replicas)
        small_copy(replica, other).wait_send()
        small_copy(other, replica).wait_recv()
    summed = small[0]
    for r in range(1, replicas):
        summed = summed + small[r]
    for slot in range(loops):
        gb[slot] = summed[slot : slot + 1, :]
    loss[...] = summed[loops : loops + 1, :128] / total


def local(
    features,
    positions,
    labels,
    cross_u,
    cross_v,
    cross_bias,
    head,
    pos_table,
    debias_hidden_weight,
    debias_tower_bias,
    debias_output_weight,
):
    micro, rows, width = features.shape
    loops, _, _, rank = cross_u.shape
    total = micro * rows * lax.axis_size("rep")
    bf16, f32 = jnp.bfloat16, jnp.float32
    vmem = pl.BlockSpec(memory_space=pltpu.VMEM)
    act = pltpu.VMEM((loops, micro, rows, width), bf16)
    wide = pltpu.VMEM((loops, micro * rows, width), bf16)
    thin = pltpu.VMEM((loops, micro * rows, rank), bf16)
    grad_u = pltpu.VMEM((loops, width, rank), bf16)
    grad_v = pltpu.VMEM((loops, rank, width), bf16)
    rep_sems = pltpu.SemaphoreType.DMA((2, loops * PARTS))
    replicas = lax.axis_size("rep")
    sems = pltpu.SemaphoreType.DMA((loops, micro))
    gu, gv, gb, loss = pl.pallas_call(
        functools.partial(kernel, float(total)),
        out_shape=(
            jax.ShapeDtypeStruct((loops, width, rank), bf16),
            jax.ShapeDtypeStruct((loops, rank, width), bf16),
            jax.ShapeDtypeStruct(cross_bias.shape, f32),
            jax.ShapeDtypeStruct((1, 128), f32),
        ),
        in_specs=[vmem] * 11,
        out_specs=(vmem,) * 4,
        scratch_shapes=[
            act,
            act,
            wide,
            thin,
            pltpu.VMEM((loops, micro, rows, 1), f32),
            act,
            act,
            wide,
            thin,
            pltpu.VMEM((micro, rows, 1), f32),
            pltpu.VMEM((micro, rows, 1), f32),
            pltpu.VMEM((rows, 1), f32),
            sems,
            sems,
            sems,
            sems,
            grad_u,
            grad_v,
            grad_u,
            grad_v,
            grad_u,
            grad_v,
            rep_sems,
            rep_sems,
            rep_sems,
            rep_sems,
            pltpu.VMEM((8, 128), f32),
            pltpu.SemaphoreType.DMA,
            pltpu.SemaphoreType.DMA,
            pltpu.VMEM((replicas, loops + 1, width), f32),
            pltpu.SemaphoreType.DMA((replicas,)),
            pltpu.SemaphoreType.DMA((replicas,)),
        ],
        compiler_params=pltpu.CompilerParams(
            collective_id=0, has_side_effects=True, vmem_limit_bytes=56 * 2**20
        ),
    )(
        features,
        positions,
        labels,
        cross_u,
        cross_v,
        cross_bias,
        head[None, :],
        pos_table,
        debias_hidden_weight,
        debias_tower_bias[None, :],
        debias_output_weight[None, :],
    )
    return (loss[0, 0], gu.astype(f32)[:, None], gv.astype(f32)[:, None], gb)


def solution(mesh):
    return jax.shard_map(
        local,
        mesh=mesh,
        in_specs=(
            P(None, "rep", None),
            P(None, "rep"),
            P(None, "rep"),
            P(None, "section", None, None),
            P(None, "section", None, None),
            P(None, "section", None),
            P(),
            P(),
            P(),
            P(),
            P(),
        ),
        out_specs=(
            P(),
            P(None, "section", None, None),
            P(None, "section", None, None),
            P(None, "section", None),
        ),
        check_vma=False,
    )
```

```python
import functools

import jax
import jax.numpy as jnp
from jax import lax
from jax.experimental import pallas as pl
from jax.experimental.pallas import tpu as pltpu
from jax.sharding import PartitionSpec as P

EPS = 1e-05
PARTS = 16
MESH = pl.DeviceIdType.MESH
NN = (((1,), (0,)), ((), ()))
NT = (((1,), (1,)), ((), ()))
TN = (((0,), (0,)), ((), ()))


def dot(a, b, dims):
    return lax.dot_general(a, b, dims, preferred_element_type=jnp.float32)


def kernel(
    total,
    feat,
    pos,
    lab,
    u,
    v,
    bias,
    head,
    table,
    hidden_w,
    tower_b,
    out_w,
    gu,
    gv,
    gb,
    loss,
    xs,
    outs,
    normed,
    inner,
    scales,
    gs,
    gouts,
    gcross,
    ginner,
    tower,
    labcol,
    loss_rows,
    fsend,
    frecv,
    bsend,
    brecv,
    own_u,
    own_v,
    part_u,
    part_v,
    inn_u,
    inn_v,
    asend,
    precv,
    osend,
    irecv,
    loss_in,
    lsend,
    lrecv,
    small,
    ssend,
    srecv,
):
    micro, rows, width = feat.shape
    loops = u.shape[0]
    sections = lax.axis_size("section")
    section = lax.axis_index("section")
    after = lax.rem(section + 1, sections)
    before = lax.rem(section + sections - 1, sections)
    is_first = section == 0
    is_last = section == sections - 1
    first = jnp.where(is_first, 1, 0)
    last = jnp.where(is_last, 1, 0)

    barrier = pltpu.get_barrier_semaphore()
    for neighbour in (before, after):
        pl.semaphore_signal(
            barrier, inc=1, device_id={"section": neighbour}, device_id_type=MESH
        )
    replicas = lax.axis_size("rep")
    replica = lax.axis_index("rep")
    for step in range(1, replicas):
        pl.semaphore_signal(
            barrier,
            inc=1,
            device_id={"rep": lax.rem(replica + step, replicas)},
            device_id_type=MESH,
        )

    @pl.when(is_first)
    def _():
        xs[0] = feat[...]

    @pl.when(is_last)
    def _():
        hidden = jax.nn.relu(
            lax.dot_general(
                table[...],
                hidden_w[...],
                NN,
                precision=lax.Precision.HIGHEST,
                preferred_element_type=jnp.float32,
            )
            + tower_b[...]
        )
        by_pos = jnp.sum(hidden * out_w[...], axis=1, keepdims=True)
        places = by_pos.shape[0]
        square = (rows, rows)
        eye = lax.broadcasted_iota(jnp.int32, square, 0) == lax.broadcasted_iota(
            jnp.int32, square, 1
        )
        ids = lax.broadcasted_iota(jnp.int32, (places, rows), 0)
        for m in range(micro):
            row = jnp.sum(
                jnp.where(ids == pos[m : m + 1, :], by_pos, 0.0), axis=0, keepdims=True
            )
            tower[m] = jnp.sum(jnp.where(eye, row, 0.0), axis=1, keepdims=True)
            labf = lab[m : m + 1, :].astype(jnp.float32)
            labcol[m] = jnp.sum(jnp.where(eye, labf, 0.0), axis=1, keepdims=True)

    loss_rows[...] = jnp.zeros_like(loss_rows)
    pl.semaphore_wait(barrier, 1 + replicas)

    def forward_copy(slot, m, to_slot):
        return pltpu.make_async_remote_copy(
            src_ref=outs.at[slot, m],
            dst_ref=xs.at[to_slot, m],
            send_sem=fsend.at[slot, m],
            recv_sem=frecv.at[to_slot, m],
            device_id={"section": after},
            device_id_type=MESH,
        )

    def backward_copy(slot, m, to_slot):
        return pltpu.make_async_remote_copy(
            src_ref=gouts.at[slot, m],
            dst_ref=gs.at[to_slot, m],
            send_sem=bsend.at[slot, m],
            recv_sem=brecv.at[to_slot, m],
            device_id={"section": before},
            device_id_type=MESH,
        )

    def rows_of(m):
        return pl.ds(pl.multiple_of(m * rows, rows), rows)

    def backward(slot, m):
        g = gs[slot, m].astype(jnp.float32)
        gc = (g * feat[m].astype(jnp.float32)).astype(jnp.bfloat16)
        gcross[slot, rows_of(m), :] = gc
        gi = dot(gc, v[slot, 0], NT).astype(jnp.bfloat16)
        ginner[slot, rows_of(m), :] = gi

        @pl.when(jnp.logical_not(is_first & (slot == 0)))
        def _():
            gn = dot(gi, u[slot, 0], NT)
            xf = xs[slot, m].astype(jnp.float32)
            scale = scales[slot, m]
            inside = jnp.mean(gn * xf, axis=-1, keepdims=True)
            gin = g + scale * gn - xf * (scale * scale * scale * inside)
            gouts[slot, m] = gin.astype(jnp.bfloat16)
            backward_copy(slot, m, slot - first).start()

    def forward(t, carry):
        slot, m = t // micro, t % micro

        @pl.when(jnp.logical_not(is_first & (slot == 0)))
        def _():
            forward_copy(slot, m, slot).wait_recv()

        xf = xs[slot, m].astype(jnp.float32)
        scale = lax.rsqrt(jnp.mean(xf * xf, axis=-1, keepdims=True) + EPS)
        scales[slot, m] = scale
        nm = (xf * scale).astype(jnp.bfloat16)
        normed[slot, rows_of(m), :] = nm
        mid = dot(nm, u[slot, 0], NN).astype(jnp.bfloat16)
        inner[slot, rows_of(m), :] = mid
        cross = dot(mid, v[slot, 0], NN) + bias[slot]
        out = (xf + feat[m].astype(jnp.float32) * cross).astype(jnp.bfloat16)
        ends = is_last & (slot == loops - 1)

        @pl.when(jnp.logical_not(ends))
        def _():
            outs[slot, m] = out
            forward_copy(slot, m, slot + last).start()

        @pl.when(ends)
        def _():
            logit = (
                jnp.sum(out.astype(jnp.float32) * head[...], axis=-1, keepdims=True)
                + tower[m]
            )
            labf = labcol[m]
            soft = jnp.maximum(logit, 0.0) + jnp.log1p(jnp.exp(-jnp.abs(logit)))
            loss_rows[...] += soft - labf * logit
            dlogit = (1.0 / (1.0 + jnp.exp(-logit)) - labf) / total
            gs[slot, m] = (dlogit * head[...]).astype(jnp.bfloat16)
            backward(slot, m)

        return carry

    lax.fori_loop(0, loops * micro, forward, 0)

    middle_left = (replicas - 1) // 2
    middle_right = middle_left + 1
    on_left = replica <= middle_left
    in_middle = (replica == middle_left) | (replica == middle_right)
    inward = jnp.where(on_left, replica + 1, replica - 1)
    has_outward = (replica > 0) & (replica < replicas - 1)
    outward = jnp.where(on_left, replica - 1, replica + 1)
    outward = jnp.clip(outward, 0, replicas - 1)
    pieces = loops * PARTS
    rank = own_v.shape[1]
    tall_u, tall_v = width // PARTS, rank // PARTS
    at_end = jnp.logical_not(has_outward | in_middle)
    early = jnp.where(at_end, 1, 2)
    lag = jnp.where(in_middle, 6, 9)

    def piece(ref, kind, q):
        tall = (tall_u, tall_v)[kind]
        slot, p = loops - 1 - q // PARTS, q % PARTS
        return ref.at[slot, pl.ds(pl.multiple_of(p * tall, tall), tall), :]

    def rep_copy(kind, q, source, target, send, recv, to):
        return pltpu.make_async_remote_copy(
            src_ref=piece(source, kind, q),
            dst_ref=piece(target, kind, q),
            send_sem=send.at[kind, q],
            recv_sem=recv.at[kind, q],
            device_id={"rep": to},
            device_id_type=MESH,
        )

    own, part, inn, done = (own_u, own_v), (part_u, part_v), (inn_u, inn_v), (gu, gv)

    def to_middle(kind, q):
        return rep_copy(kind, q, own[kind], part[kind], asend, precv, inward)

    def across(kind, q):
        return rep_copy(kind, q, own[kind], inn[kind], asend, irecv, inward)

    def to_ends(kind, q):
        return rep_copy(kind, q, done[kind], inn[kind], osend, irecv, outward)

    def add(a, b):
        return (a.astype(jnp.float32) + b.astype(jnp.float32)).astype(jnp.bfloat16)

    def gather_in(q):
        for kind in range(2):

            @pl.when(has_outward)
            def _(kind=kind):
                to_middle(kind, q).wait_recv()
                mine = piece(own[kind], kind, q)
                mine[...] = add(mine[...], piece(part[kind], kind, q)[...])

            @pl.when(in_middle)
            def _(kind=kind):
                across(kind, q).start()

            @pl.when(jnp.logical_not(in_middle))
            def _(kind=kind):
                to_middle(kind, q).start()

    def give_out(q):
        for kind in range(2):
            across(kind, q).wait_recv()
            arrived = piece(inn[kind], kind, q)[...]
            result = piece(done[kind], kind, q)

            @pl.when(in_middle)
            def _(kind=kind, arrived=arrived, result=result):
                result[...] = add(piece(own[kind], kind, q)[...], arrived)

            @pl.when(jnp.logical_not(in_middle))
            def _(arrived=arrived, result=result):
                result[...] = arrived

            @pl.when(has_outward)
            def _(kind=kind):
                to_ends(kind, q).start()

    def reduce_step(t, ahead=False):
        gathers = (t >= early) & (t - early < pieces)

        @pl.when(gathers & jnp.logical_not(at_end) if ahead else gathers)
        def _():
            gather_in(t - early)

        @pl.when((t >= lag) & (t - lag < pieces))
        def _():
            give_out(t - lag)

    def send_ahead(start, stop):
        @pl.when(at_end)
        def _():
            def one(q, carry):
                for kind in range(2):
                    to_middle(kind, q).start()
                return carry

            lax.fori_loop(start, stop, one, 0)

    chunks = 4
    chunk = width // chunks

    def weight_grads(slot, then=None):
        def some(c, carry):
            cols = pl.ds(pl.multiple_of(c * chunk, chunk), chunk)
            own_u[slot, cols, :] = dot(normed[slot, :, cols], ginner[slot], TN).astype(
                jnp.bfloat16
            )
            gc = gcross[slot, :, cols]
            own_v[slot, :, cols] = dot(inner[slot], gc, TN).astype(jnp.bfloat16)
            small[replica, slot : slot + 1, cols] = jnp.sum(
                gc.astype(jnp.float32), axis=0, keepdims=True
            )
            if then is not None:
                then(c)
            return carry

        lax.fori_loop(0, chunks, some, 0)

    def loss_copy():
        return pltpu.make_async_remote_copy(
            src_ref=loss_in,
            dst_ref=loss_in,
            send_sem=lsend,
            recv_sem=lrecv,
            device_id={"section": before},
            device_id_type=MESH,
        )

    def small_copy(source, to):
        return pltpu.make_async_remote_copy(
            src_ref=small.at[source],
            dst_ref=small.at[source],
            send_sem=ssend.at[to],
            recv_sem=srecv.at[source],
            device_id={"rep": to},
            device_id_type=MESH,
        )

    beside = loops > 1 and micro + chunks <= PARTS
    for back in range(loops):
        slot = loops - 1 - back

        def step(m, carry, slot=slot, back=back):
            ends = is_last & (slot == loops - 1)

            @pl.when(jnp.logical_not(ends))
            def _():
                backward_copy(slot, m, slot).wait_recv()
                backward(slot, m)

            if back > 0 and beside:
                reduce_step((back - 1) * micro + m)
            return carry

        lax.fori_loop(0, micro, step, 0)
        if back == 0:

            @pl.when(is_last)
            def _():
                loss_in[...] = jnp.broadcast_to(
                    jnp.sum(loss_rows[...], keepdims=True), loss_in.shape
                )

            @pl.when(jnp.logical_not(is_last))
            def _():
                loss_copy().wait_recv()

            @pl.when(jnp.logical_not(is_first))
            def _():
                loss_copy().start()

        if slot > 0:
            weight_grads(slot)

    now = (loops - 1) * micro if beside else 0
    begin = max(now - 1, 0)
    split = pieces - PARTS
    send_ahead(begin, split)
    if loops > 1:
        weight_grads(0, lambda c: reduce_step(now + c, ahead=True))
        now = now + chunks
    else:
        weight_grads(0)
    send_ahead(split, pieces)
    small[replica, loops : loops + 1, :] = jnp.broadcast_to(loss_in[:1, :1], (1, width))
    for step in range(1, replicas):
        small_copy(replica, lax.rem(replica + step, replicas)).start()

    def tail(t, carry):
        reduce_step(t, ahead=True)
        return carry

    lax.fori_loop(now, pieces + 9, tail, 0)

    def drain(t, carry):
        slot, m = t // micro, t % micro

        @pl.when(jnp.logical_not(is_last & (slot == loops - 1)))
        def _():
            forward_copy(slot, m, slot).wait_send()

        @pl.when(jnp.logical_not(is_first & (slot == 0)))
        def _():
            backward_copy(slot, m, slot).wait_send()

        return carry

    lax.fori_loop(0, loops * micro, drain, 0)

    def drain_rep(q, carry):
        for kind in range(2):
            across(kind, q).wait_send()

            @pl.when(has_outward)
            def _(kind=kind):
                to_ends(kind, q).wait_send()

        return carry

    lax.fori_loop(0, pieces, drain_rep, 0)

    @pl.when(jnp.logical_not(is_first))
    def _():
        loss_copy().wait_send()

    for step in range(1, replicas):
        other = lax.rem(replica + step, replicas)
        small_copy(replica, other).wait_send()
        small_copy(other, replica).wait_recv()
    summed = small[0]
    for r in range(1, replicas):
        summed = summed + small[r]
    for slot in range(loops):
        gb[slot] = summed[slot : slot + 1, :]
    loss[...] = summed[loops : loops + 1, :128] / total


def local(
    features,
    positions,
    labels,
    cross_u,
    cross_v,
    cross_bias,
    head,
    pos_table,
    debias_hidden_weight,
    debias_tower_bias,
    debias_output_weight,
):
    micro, rows, width = features.shape
    loops, _, _, rank = cross_u.shape
    total = micro * rows * lax.axis_size("rep")
    bf16, f32 = jnp.bfloat16, jnp.float32
    vmem = pl.BlockSpec(memory_space=pltpu.VMEM)
    act = pltpu.VMEM((loops, micro, rows, width), bf16)
    wide = pltpu.VMEM((loops, micro * rows, width), bf16)
    thin = pltpu.VMEM((loops, micro * rows, rank), bf16)
    grad_u = pltpu.VMEM((loops, width, rank), bf16)
    grad_v = pltpu.VMEM((loops, rank, width), bf16)
    rep_sems = pltpu.SemaphoreType.DMA((2, loops * PARTS))
    replicas = lax.axis_size("rep")
    sems = pltpu.SemaphoreType.DMA((loops, micro))
    gu, gv, gb, loss = pl.pallas_call(
        functools.partial(kernel, float(total)),
        out_shape=(
            jax.ShapeDtypeStruct((loops, width, rank), bf16),
            jax.ShapeDtypeStruct((loops, rank, width), bf16),
            jax.ShapeDtypeStruct(cross_bias.shape, f32),
            jax.ShapeDtypeStruct((1, 128), f32),
        ),
        in_specs=[vmem] * 11,
        out_specs=(vmem,) * 4,
        scratch_shapes=[
            act,
            act,
            wide,
            thin,
            pltpu.VMEM((loops, micro, rows, 1), f32),
            act,
            act,
            wide,
            thin,
            pltpu.VMEM((micro, rows, 1), f32),
            pltpu.VMEM((micro, rows, 1), f32),
            pltpu.VMEM((rows, 1), f32),
            sems,
            sems,
            sems,
            sems,
            grad_u,
            grad_v,
            grad_u,
            grad_v,
            grad_u,
            grad_v,
            rep_sems,
            rep_sems,
            rep_sems,
            rep_sems,
            pltpu.VMEM((8, 128), f32),
            pltpu.SemaphoreType.DMA,
            pltpu.SemaphoreType.DMA,
            pltpu.VMEM((replicas, loops + 1, width), f32),
            pltpu.SemaphoreType.DMA((replicas,)),
            pltpu.SemaphoreType.DMA((replicas,)),
        ],
        compiler_params=pltpu.CompilerParams(
            collective_id=0, has_side_effects=True, vmem_limit_bytes=56 * 2**20
        ),
    )(
        features,
        positions,
        labels,
        cross_u,
        cross_v,
        cross_bias,
        head[None, :],
        pos_table,
        debias_hidden_weight,
        debias_tower_bias[None, :],
        debias_output_weight[None, :],
    )
    return (loss[0, 0], gu.astype(f32)[:, None], gv.astype(f32)[:, None], gb)


def solution(mesh):
    return jax.shard_map(
        local,
        mesh=mesh,
        in_specs=(
            P(None, "rep", None),
            P(None, "rep"),
            P(None, "rep"),
            P(None, "section", None, None),
            P(None, "section", None, None),
            P(None, "section", None),
            P(),
            P(),
            P(),
            P(),
            P(),
        ),
        out_specs=(
            P(),
            P(None, "section", None, None),
            P(None, "section", None, None),
            P(None, "section", None),
        ),
        check_vma=False,
    )
```
